32 devices in a mesh: groups: 2 (over y), expert: 16 (over z, x, core), dp: 1.
Axes of the slice: x: 2, y: 2, z: 4, core: 2. Of those that a mesh axis runs over, the one named last changes fastest.
Arguments:
- cotangent: bfloat16 [4096, 4096], P(('groups', 'expert', 'dp')), parts along dimension 0, may hold values from -6 to 6
- hidden: bfloat16 [4096, 8, 768], P(('groups', 'expert', 'dp')), parts along dimension 0, may hold values from -6 to 6
- gates: bfloat16 [4096, 8], P(('groups', 'expert', 'dp')), parts along dimension 0, may hold values from 0.099609375 to 1
- expert_ids: int32 [4096, 8], P(('groups', 'expert', 'dp')), parts along dimension 0, may hold values from 0 to 15, all different within a row; in each aligned block of 128 rows (0 to 127, 128 to 255, ...) at most 80 rows name the same one
- counts: int32 [32], P(('groups', 'expert', 'dp')), parts along dimension 0, may hold values from 32 to 128
- proj_out: bfloat16 [64, 4096], P(None, 'dp'), may hold values from -0.09375 to 0.09375
- proj_in: bfloat16 [16, 64, 768], P('expert', None, 'dp'), may hold values from -0.21875 to 0.21875
Outputs:
- grads: bfloat16 [32, 16, 4096], P(('groups', 'expert', 'dp')), parts along dimension 0
The draws below stay inside these ranges and needn't reach their ends.
There are 2 independent parts, one for each index of `groups`. The reference program is written for one: setup_inputs(seed, part) draws one part's arguments, and reference() takes and returns one part's arrays. A program takes and returns all parts, laid end to end along the dimension named above; an argument that names none is the same for every part. Nothing has to cross between parts.
Inputs may be any that keep to these rules, and one draw needn't show every extreme that they name: `expert_ids`: each row names 8 different experts. Among the 128 rows of one device, no expert is named more than 80 times, a bound that some block reaches.
All inputs are finite; a program needn't handle non-finite values.
Results may differ from the reference program's by a relative error of at most 0.0057.
Values may be sent and summed in bfloat16 or wider, within the bound.
A program may use at most 64 MiB of HBM per device.

```python
import math
from functools import partial
import jax
import jax.numpy as jnp
import numpy as np
from jax import lax

D = 4096
TOP = 8
FFW = 768
R = 64
SEQ = 128
TOK_DEV = 128
EXPERTS = 16
EXAMPLES = 16
TOKENS = 2048
CAP = 80


def set_ends(values, key, low, high):
    index_at = [jax.random.randint(jax.random.fold_in(key, axis), (), 0, length) for axis, length in enumerate(values.shape)]
    main_axis = values.shape.index(max(values.shape))
    beside = index_at[:main_axis] + [(index_at[main_axis] + 1) % values.shape[main_axis]] + index_at[main_axis + 1:]
    return values.at[tuple(index_at)].set(low).at[tuple(beside)].set(high)


def block_levels(stream_key, extent, split, smallest, top_value):
    factor_of = 1.0
    for dim, parts in split:
        heights = jax.random.uniform(jax.random.fold_in(jax.random.fold_in(stream_key, 6), dim), (parts,), jnp.float32, smallest / len(split), top_value / len(split))
        factor_of = factor_of * jnp.repeat(jnp.exp(heights), extent[dim] // parts).reshape((-1,) + (1,) * (len(extent) - 1 - dim))
    return factor_of


def shared_out(rng, own, number, rows, number_of, top, limit, skew):
    sequence = jax.random.permutation(rng, number_of)
    crowded, ordinary = load_shares(number_of, rows * top, limit, skew, True), load_shares(number_of, rows * top, limit, skew, False)
    places = jnp.arange(number_of)

    def named(lengths, offset_by):
        used = int((lengths > 0).sum())
        fixed = max(1, used // 4)
        moved = fixed + (places - fixed + offset_by * (used - fixed)) % max(1, number_of - fixed)
        return jnp.zeros((number_of,), jnp.int32).at[sequence[jnp.where(places < fixed, places, moved)]].set(jnp.asarray(lengths, jnp.int32))

    lengths = jnp.where(number % 4 == 0, named(crowded, number // 4), named(ordinary, number - number // 4 - 1))
    mixed = jax.random.permutation(jax.random.fold_in(own, 3), number_of)
    source_of, receiver = mixed[0:number_of // 2 * 2:2], mixed[1:number_of // 2 * 2:2]
    margin = jnp.minimum(lengths[source_of] - 1, limit - lengths[receiver]) // 2
    margin = jnp.where((source_of == sequence[0]) | (receiver == sequence[0]) | (lengths[receiver] == 0), 0, jnp.maximum(margin, 0))
    moved = jax.random.randint(jax.random.fold_in(own, 4), (number_of // 2,), 0, 1 << 20) % (margin + 1)
    lengths = lengths.at[source_of].add(-moved).at[receiver].add(moved)
    items = jnp.searchsorted(jnp.cumsum(lengths), jnp.arange(rows * top), side="right").astype(jnp.int32)
    listing = items.reshape(top, rows).T
    listing = listing[jax.random.permutation(jax.random.fold_in(own, 1), rows)]
    offset_by = jax.random.randint(jax.random.fold_in(own, 2), (rows, 1), 0, top)
    return jnp.take_along_axis(listing, (jnp.arange(top)[None, :] + offset_by) % top, axis=1)


def load_shares(number_of, total, most, lean, full):
    portions = [(1 << 20) // math.isqrt(standing ** lean) + 1 for standing in range(1, number_of + 1)]
    largest = most if full else min(most, max(-(-total // number_of), total * portions[0] // sum(portions)))
    least = 1 if total - largest >= number_of - 1 else 0
    given, rest = [largest] + [least] * (number_of - 1), total - largest - least * (number_of - 1)
    while rest > 0:
        free = [i for i in range(1, number_of) if given[i] < largest] or [i for i in range(1, number_of) if given[i] < most]
        pool, remaining = sum([portions[i] for i in free]), rest
        for i in free:
            extra = min(most - given[i], max(1, remaining * portions[i] // pool), rest)
            given[i] = given[i] + extra
            rest = rest - extra
    return np.array(given)


def normal_values(rng, shape, deviation, most, split=(), kind=jnp.bfloat16):
    drawn = jax.random.normal(rng, shape, jnp.float32) * deviation
    if len(split) > 0:
        drawn = block_levels(rng, shape, split, -0.22, 0.18) * drawn
    return jnp.clip(drawn, min=-most, max=most).astype(kind)


def setup_inputs(seed: int = 0, part: int = 0) -> dict:
    key_list = jax.random.split(jax.random.key(seed), 8)
    part_splits = jax.random.split(jax.random.fold_in(key_list[7], part), 8)
    cotangent = normal_values(part_splits[0], (TOKENS, D), 1.0, 6.0, ((0, 16),))
    hidden = normal_values(part_splits[1], (TOKENS, TOP, FFW), 1.0, 6.0, ((0, 16),))
    gates = jnp.clip(0.099609375 + 0.9003906 * jax.random.uniform(part_splits[2], (TOKENS, TOP), jnp.float32) ** block_levels(part_splits[2], (TOKENS, TOP), ((0, 16),), -0.2, 0.2), 0.099609375, 1.0).astype(jnp.bfloat16)
    expert_ids_keys = jax.random.split(jax.random.fold_in(part_splits[3], 1), TOKENS // TOK_DEV)
    expert_ids_turns = jax.random.permutation(jax.random.fold_in(part_splits[3], 3), TOKENS // TOK_DEV)
    expert_ids = jax.vmap(lambda own, number: shared_out(jax.random.fold_in(part_splits[3], 2), own, number, TOK_DEV, EXPERTS, TOP, CAP, 2))(expert_ids_keys, expert_ids_turns).reshape((TOKENS, TOP))
    counts = set_ends(jax.random.randint(part_splits[4], (EXAMPLES,), SEQ // 4, SEQ + 1), jax.random.fold_in(part_splits[4], 1), SEQ // 4, SEQ).astype(jnp.int32)
    proj_out = normal_values(key_list[5], (R, D), D ** -0.5, 0.09375)
    proj_in = normal_values(key_list[6], (EXPERTS, R, FFW), FFW ** -0.5, 0.21875, ((0, 16),))
    return dict(cotangent=cotangent, hidden=hidden, gates=gates, expert_ids=expert_ids, counts=counts, proj_out=proj_out, proj_in=proj_in)


def reduce_block(operands, basis_all):
    block_rows, block_ids = operands
    expert_hot = (block_ids[:, None] == jnp.arange(EXPERTS, dtype=jnp.int32)[None, :]).astype(jnp.int32)
    earlier = jnp.cumsum(expert_hot, axis=0) - expert_hot
    target = (block_ids * CAP + jnp.sum(earlier * expert_hot, axis=1)).astype(jnp.int32)
    placed = jnp.zeros((EXPERTS * CAP, FFW), jnp.float32).at[target].set(block_rows.astype(jnp.float32))
    product = jnp.einsum("ejf,erf->ejr", placed.reshape(EXPERTS, CAP, FFW), basis_all)
    return product.reshape(EXPERTS * CAP, R)[target].astype(jnp.bfloat16)


def example_block(operands):
    scaled, reduced, block_ids = operands
    outer_terms = scaled.astype(jnp.float32)[:, :, None] * reduced.astype(jnp.float32)[:, None, :]
    summed = jnp.zeros((EXPERTS, R, R), jnp.float32).at[block_ids].add(outer_terms)
    return summed.reshape(EXPERTS, R * R).astype(jnp.bfloat16)


def reference(cotangent, hidden, gates, expert_ids, counts, proj_out, proj_in):
    position = jnp.arange(TOKENS, dtype=jnp.int32)
    live_mask = (position % SEQ < counts[position // SEQ]).astype(jnp.float32)
    projected = jnp.dot(cotangent, proj_out.T, preferred_element_type=jnp.float32)
    weights = gates.astype(jnp.float32) * live_mask[:, None]
    scaled = (weights[:, :, None] * projected[:, None, :]).astype(jnp.bfloat16)
    basis_all = proj_in.astype(jnp.float32)
    blocks = TOKENS // TOK_DEV
    reduced = lax.map(partial(reduce_block, basis_all=basis_all),
                      (hidden.reshape(blocks, TOK_DEV * TOP, FFW), expert_ids.reshape(blocks, TOK_DEV * TOP)))
    grads = lax.map(example_block,
                    (scaled.reshape(EXAMPLES, SEQ * TOP, R), reduced.reshape(EXAMPLES, SEQ * TOP, R),
                     expert_ids.reshape(EXAMPLES, SEQ * TOP)))
    return grads
```

```python
import functools

import jax
import jax.numpy as jnp
from jax import lax
from jax.experimental import pallas as pl
from jax.experimental.pallas import tpu as pltpu
from jax.sharding import PartitionSpec as P

ACROSS = (((1,), (1,)), ((), ()))


def route_columns(cot, basis_out, gates, ids, used):
    top, tokens = gates.shape
    routes = tokens * top
    rank = basis_out.shape[0]
    projected = lax.dot_general(cot, basis_out, ACROSS, preferred_element_type=jnp.float32)
    spread = (
        lax.broadcasted_iota(jnp.int32, (routes, tokens), 0) // top
        == lax.broadcasted_iota(jnp.int32, (routes, tokens), 1)
    ).astype(jnp.bfloat16)
    own = lax.broadcasted_iota(jnp.int32, (routes, top), 0) % top == lax.broadcasted_iota(
        jnp.int32, (routes, top), 1
    )

    def column(values):
        wide = lax.dot_general(spread, values, ACROSS, preferred_element_type=jnp.float32)
        return jnp.sum(jnp.where(own, wide, 0.0), axis=1, keepdims=True)

    gate = column(gates)
    expert = column(ids.astype(jnp.float32).astype(jnp.bfloat16))
    live = lax.broadcasted_iota(jnp.int32, (routes, 1), 0) // top < used
    weight = jnp.where(live, gate, 0.0)
    rows = jnp.broadcast_to(projected[:, None, :], (tokens, top, rank)).reshape(routes, rank)
    scaled = weight * rows
    return scaled.T.astype(jnp.bfloat16), jnp.broadcast_to(expert, (routes, 2 * rank))


def pair_sums(first, hidden, basis_pair, scaled_t, expert, acc_ref):
    rank = basis_pair.shape[0] // 2
    routes = hidden.shape[0]
    reduced = lax.dot_general(hidden, basis_pair, ACROSS, preferred_element_type=jnp.float32)
    lane = lax.broadcasted_iota(jnp.int32, (routes, 2 * rank), 1)
    names = (first + lane // rank).astype(jnp.float32)
    kept = jnp.where(expert == names, reduced, 0.0).astype(jnp.bfloat16)
    sums = jnp.dot(scaled_t, kept, preferred_element_type=jnp.float32)
    turned = pltpu.roll(sums, rank, 1)
    left = lax.broadcasted_iota(jnp.int32, (rank, 2 * rank), 1) < rank
    at = pl.multiple_of(first * rank, 2 * rank)
    acc_ref[pl.ds(at, rank), :] = jnp.where(left, sums, turned)
    acc_ref[pl.ds(at + rank, rank), :] = jnp.where(left, turned, sums)


def write_out(acc_ref, out_ref, rank):
    experts = out_ref.shape[1]
    left = lax.broadcasted_iota(jnp.int32, (experts, 2 * rank), 1) < rank
    for c in range(rank // 2):
        even = acc_ref[pl.ds(2 * c, experts, stride=rank), :]
        odd = acc_ref[pl.ds(2 * c + 1, experts, stride=rank), :]
        out_ref[0, :, pl.ds(c * 2 * rank, 2 * rank)] = jnp.where(left, even, odd).astype(out_ref.dtype)


def ring_kernel(
    parts,
    counts_ref, cot_ref, hidden_ref, gates_ref, ids_ref, out_basis_ref, in_basis_ref,
    out_ref,
    counts, cot, hidden, gates, ids, out_basis, basis, scaled_t, expert, acc,
    load_sem, z_send, z_recv, x_send, x_recv, c_send, c_recv,
):
    nz, nx, nc = parts
    rank, width = in_basis_ref.shape
    me = lax.axis_index("expert")
    z, x, c = me // (nx * nc), (me // nc) % nx, me % nc

    def place(pz, px, pc):
        return (pz * nx + px) * nc + pc

    def slot(e):
        return basis.at[pl.ds(pl.multiple_of(e * rank, rank), rank), :]

    loads = [
        pltpu.make_async_copy(src, dst, load_sem.at[i])
        for i, (src, dst) in enumerate(
            [
                (in_basis_ref, slot(me)),
                (cot_ref, cot),
                (out_basis_ref, out_basis),
                (gates_ref, gates),
                (ids_ref, ids),
                (counts_ref, counts),
                (hidden_ref, hidden),
            ]
        )
    ]
    for load in loads:
        load.start()

    x_peer, c_peer = place(z, 1 - x, c), place(z, x, 1 - c)
    peers = [place((z + s) % nz, x, c) for s in range(1, nz)] + [x_peer, c_peer]
    barrier = pltpu.get_barrier_semaphore()
    for peer in peers:
        pl.semaphore_signal(
            barrier, inc=1, device_id={"expert": peer}, device_id_type=pl.DeviceIdType.MESH
        )
    pl.semaphore_wait(barrier, len(peers))

    def send(source, e, peer, send_sem, recv_sem):
        copy = pltpu.make_async_remote_copy(
            src_ref=source,
            dst_ref=slot(e),
            send_sem=send_sem,
            recv_sem=recv_sem,
            device_id={"expert": peer},
            device_id_type=pl.DeviceIdType.MESH,
        )
        copy.start()
        return copy

    column = [place((z - s + nz) % nz, x, c) for s in range(nz)]
    across = [place((z - s + nz) % nz, 1 - x, c) for s in range(nz)]
    z_copy, x_copy, c_copy = {}, {}, {}
    order = [1, 3, 2] if nz == 4 else list(range(1, nz))
    for s in order:
        z_copy[s] = send(in_basis_ref, me, place((z + s) % nz, x, c), z_send.at[s - 1], z_recv.at[s - 1])
    x_copy[0] = send(in_basis_ref, me, x_peer, x_send.at[0], x_recv.at[0])
    c_copy[0] = send(in_basis_ref, me, c_peer, c_send.at[0], c_recv.at[0])

    for load in loads[1:6]:
        load.wait()
    scaled_t[...], expert[...] = route_columns(
        cot[...], out_basis[...], gates[...], ids[...], counts[0]
    )
    loads[6].wait()
    loads[0].wait()

    def pair(e):
        first = e // 2 * 2
        pair_sums(
            first,
            hidden[...],
            basis[pl.ds(pl.multiple_of(first * rank, 2 * rank), 2 * rank), :],
            scaled_t[...],
            expert[...],
            acc,
        )

    for s in order:
        z_copy[s].wait_recv()
        x_copy[s] = send(slot(column[s]), column[s], x_peer, x_send.at[s], x_recv.at[s])
        c_copy[s] = send(slot(column[s]), column[s], c_peer, c_send.at[s], c_recv.at[s])
    for s in [0] + order:
        x_copy[s].wait_recv()
        c_copy[nz + s] = send(
            slot(across[s]), across[s], c_peer, c_send.at[nz + s], c_recv.at[nz + s]
        )
        c_copy[s].wait_recv()
        pair(column[s])
    for s in [0] + order:
        c_copy[nz + s].wait_recv()
        pair(across[s])
    write_out(acc, out_ref, rank)
    for copies in (z_copy, x_copy, c_copy):
        for copy in copies.values():
            copy.wait_send()


def local_kernel(
    counts_ref, cot, hidden, gates, ids, out_basis, basis, out_ref, scaled_t, expert, acc
):
    rank = out_basis.shape[0]
    experts = out_ref.shape[1]
    scaled_t[...], expert[...] = route_columns(
        cot[...], out_basis[...], gates[...], ids[...], counts_ref[0]
    )

    @pl.loop(0, experts // 2)
    def _(j):
        pair_sums(
            2 * j,
            hidden[...],
            basis[pl.ds(pl.multiple_of(2 * j * rank, 2 * rank), 2 * rank), :],
            scaled_t[...],
            expert[...],
            acc,
        )

    write_out(acc, out_ref, rank)


def on_device(cotangent, hidden, gates, expert_ids, counts, proj_out, proj_in):
    tokens, top = expert_ids.shape
    routes = tokens * top
    model = cotangent.shape[1]
    rank = proj_out.shape[0]
    width = hidden.shape[2]
    experts = lax.axis_size("expert")
    dp = lax.axis_size("dp")
    bf16 = jnp.bfloat16
    if dp > 1:
        proj_out = lax.all_gather(proj_out, "dp", axis=1, tiled=True)
        proj_in = lax.all_gather(proj_in, "dp", axis=2, tiled=True)
    hidden = hidden.reshape(routes, width)
    gates, expert_ids = gates.T, expert_ids.T
    out_shape = jax.ShapeDtypeStruct((1, experts, rank * rank), bf16)
    tail = [
        pltpu.VMEM((rank, routes), bf16),
        pltpu.VMEM((routes, 2 * rank), jnp.float32),
        pltpu.VMEM((experts * rank, 2 * rank), jnp.float32),
    ]
    cost = pl.CostEstimate(
        flops=2 * routes * experts * rank * (width + rank),
        bytes_accessed=2 * (tokens * model + routes * width + experts * rank * width),
        transcendentals=0,
    )
    smem = pl.BlockSpec(memory_space=pltpu.SMEM)
    vmem = pl.BlockSpec(memory_space=pltpu.VMEM)
    anywhere = pl.BlockSpec(memory_space=pl.ANY)
    if experts != 16 or dp > 1:
        basis = lax.all_gather(proj_in.reshape(rank, width), "expert", axis=0, tiled=True)
        return pl.pallas_call(
            local_kernel,
            out_shape=out_shape,
            in_specs=[smem] + [vmem] * 6,
            out_specs=vmem,
            scratch_shapes=tail,
            cost_estimate=cost,
            compiler_params=pltpu.CompilerParams(vmem_limit_bytes=48 << 20),
        )(counts, cotangent, hidden, gates, expert_ids, proj_out, basis)
    parts = (experts // 4, 2, 2)
    dma = pltpu.SemaphoreType.DMA
    nz = parts[0]
    return pl.pallas_call(
        functools.partial(ring_kernel, parts),
        out_shape=out_shape,
        in_specs=[anywhere] * 7,
        out_specs=vmem,
        scratch_shapes=[
            pltpu.SMEM((1,), jnp.int32),
            pltpu.VMEM((tokens, model), bf16),
            pltpu.VMEM((routes, width), bf16),
            pltpu.VMEM((top, tokens), bf16),
            pltpu.VMEM((top, tokens), jnp.int32),
            pltpu.VMEM((rank, model), bf16),
            pltpu.VMEM((experts * rank, width), bf16),
        ]
        + tail
        + [
            dma((7,)),
            dma((nz - 1,)),
            dma((nz - 1,)),
            dma((nz,)),
            dma((nz,)),
            dma((2 * nz,)),
            dma((2 * nz,)),
        ],
        cost_estimate=cost,
        compiler_params=pltpu.CompilerParams(
            collective_id=0, has_side_effects=True, vmem_limit_bytes=40 << 20
        ),
    )(counts, cotangent, hidden, gates, expert_ids, proj_out, proj_in.reshape(rank, width))


def solution(mesh):
    rows = ("groups", "expert", "dp")
    placed = (
        P(rows, None),
        P(rows, None, None),
        P(rows, None),
        P(rows, None),
        P(rows),
        P(None, "dp"),
        P("expert", None, "dp"),
    )
    return jax.shard_map(
        on_device,
        mesh=mesh,
        in_specs=placed,
        out_specs=P(rows, None, None),
        check_vma=False,
    )
```

```python
import functools

import jax
import jax.numpy as jnp
from jax import lax
from jax.experimental import pallas as pl
from jax.experimental.pallas import tpu as pltpu
from jax.sharding import PartitionSpec as P

ACROSS = (((1,), (1,)), ((), ()))


def route_columns(cot, basis_out, gates, ids, used):
    top, tokens = gates.shape
    routes = tokens * top
    rank = basis_out.shape[0]
    projected = lax.dot_general(cot, basis_out, ACROSS, preferred_element_type=jnp.float32)
    spread = (
        lax.broadcasted_iota(jnp.int32, (routes, tokens), 0) // top
        == lax.broadcasted_iota(jnp.int32, (routes, tokens), 1)
    ).astype(jnp.bfloat16)
    own = lax.broadcasted_iota(jnp.int32, (routes, top), 0) % top == lax.broadcasted_iota(
        jnp.int32, (routes, top), 1
    )

    def column(values):
        wide = lax.dot_general(spread, values, ACROSS, preferred_element_type=jnp.float32)
        return jnp.sum(jnp.where(own, wide, 0.0), axis=1, keepdims=True)

    gate = column(gates)
    expert = column(ids.astype(jnp.float32).astype(jnp.bfloat16))
    live = lax.broadcasted_iota(jnp.int32, (routes, 1), 0) // top < used
    weight = jnp.where(live, gate, 0.0)
    rows = jnp.broadcast_to(projected[:, None, :], (tokens, top, rank)).reshape(routes, rank)
    scaled = weight * rows
    return scaled.T.astype(jnp.bfloat16), jnp.broadcast_to(expert, (routes, 2 * rank))


def group_sums(first, hidden, basis, scaled_t, expert, acc_ref):
    rank = scaled_t.shape[0]
    routes = hidden.shape[0]
    pair = 2 * rank
    reduced = lax.dot_general(hidden, basis, ACROSS, preferred_element_type=jnp.float32)
    lane = lax.broadcasted_iota(jnp.int32, (routes, pair), 1)
    left = lax.broadcasted_iota(jnp.int32, (rank, pair), 1) < rank
    kept = []
    for p in range(basis.shape[0] // pair):
        names = (first + 2 * p + lane // rank).astype(jnp.float32)
        kept.append(jnp.where(expert == names, reduced[:, p * pair : (p + 1) * pair], 0.0))
    kept = jnp.concatenate(kept, axis=1).astype(jnp.bfloat16)
    sums = jnp.dot(scaled_t, kept, preferred_element_type=jnp.float32)
    for p in range(basis.shape[0] // pair):
        part = sums[:, p * pair : (p + 1) * pair]
        turned = pltpu.roll(part, rank, 1)
        at = pl.multiple_of((first + 2 * p) * rank, pair)
        acc_ref[pl.ds(at, rank), :] = jnp.where(left, part, turned)
        acc_ref[pl.ds(at + rank, rank), :] = jnp.where(left, turned, part)


def write_out(acc_ref, out_ref, rank):
    experts = out_ref.shape[1]
    left = lax.broadcasted_iota(jnp.int32, (experts, 2 * rank), 1) < rank
    for c in range(rank // 2):
        even = acc_ref[pl.ds(2 * c, experts, stride=rank), :]
        odd = acc_ref[pl.ds(2 * c + 1, experts, stride=rank), :]
        out_ref[0, :, pl.ds(c * 2 * rank, 2 * rank)] = jnp.where(left, even, odd).astype(out_ref.dtype)


def ring_kernel(
    parts,
    counts_ref, cot_ref, hidden_ref, gates_ref, ids_ref, out_basis_ref, in_basis_ref,
    out_ref,
    counts, cot, hidden, gates, ids, out_basis, basis, scaled_t, expert, acc,
    load_sem, z_send, z_recv, x_send, x_recv, y_send, y_recv, c_send, c_recv,
):
    nz, nx, nc = parts
    rank, width = in_basis_ref.shape
    half = rank // 2
    me = lax.axis_index("expert")
    y = lax.axis_index("groups")
    z, x, c = me // (nx * nc), (me // nc) % nx, me % nc

    def place(pz, px, pc):
        return (pz * nx + px) * nc + pc

    def whole(e):
        return basis.at[pl.ds(pl.multiple_of(e * rank, rank), rank), :]

    def piece(e, h):
        return basis.at[pl.ds(pl.multiple_of(e * rank + h * half, half), half), :]

    loads = [
        pltpu.make_async_copy(src, dst, load_sem.at[i])
        for i, (src, dst) in enumerate(
            [
                (in_basis_ref, whole(me)),
                (cot_ref, cot),
                (out_basis_ref, out_basis),
                (gates_ref, gates),
                (ids_ref, ids),
                (counts_ref, counts),
                (hidden_ref, hidden),
            ]
        )
    ]
    for load in loads:
        load.start()

    x_peer = {"expert": place(z, 1 - x, c)}
    c_peer = {"expert": place(z, x, 1 - c)}
    y_peer = {"groups": 1 - y}
    z_peer = {s: {"expert": place((z + s) % nz, x, c)} for s in range(1, nz)}
    peers = list(z_peer.values()) + [x_peer, y_peer, c_peer]
    barrier = pltpu.get_barrier_semaphore()
    for peer in peers:
        pl.semaphore_signal(barrier, inc=1, device_id=peer, device_id_type=pl.DeviceIdType.MESH)
    pl.semaphore_wait(barrier, len(peers))

    started = []

    def send(source, target, peer, sems, i):
        copy = pltpu.make_async_remote_copy(
            src_ref=source,
            dst_ref=target,
            send_sem=sems[0].at[i],
            recv_sem=sems[1].at[i],
            device_id=peer,
            device_id_type=pl.DeviceIdType.MESH,
        )
        copy.start()
        started.append(copy)
        return copy

    zs, xs, ys, cs = (z_send, z_recv), (x_send, x_recv), (y_send, y_recv), (c_send, c_recv)
    column = [place((z - s + nz) % nz, x, c) for s in range(nz)]
    across = [place((z - s + nz) % nz, 1 - x, c) for s in range(nz)]
    order = [1, 3, 2] if nz == 4 else list(range(1, nz))
    z_copy, x_copy, y_copy, c_copy = {}, {}, {}, {}

    def to_y(i, e):
        y_copy[i] = send(piece(e, y), piece(e, y), y_peer, ys, i)

    def to_c(i, e, h):
        c_copy[i] = send(piece(e, h), piece(e, h), c_peer, cs, i)

    mine = in_basis_ref.at[pl.ds(pl.multiple_of(y * half, half), half), :]
    for s in order:
        z_copy[s] = send(mine, piece(me, y), z_peer[s], zs, s - 1)
    x_copy[0] = send(in_basis_ref, whole(me), x_peer, xs, 0)
    c_copy[0] = send(in_basis_ref, whole(me), c_peer, cs, 0)

    for load in loads[1:6]:
        load.wait()
    scaled_t[...], expert[...] = route_columns(
        cot[...], out_basis[...], gates[...], ids[...], counts[0]
    )
    loads[6].wait()
    loads[0].wait()

    def quad(s):
        first = (z - s + nz) % nz * (nx * nc)
        rows = nx * nc * rank
        group_sums(
            first,
            hidden[...],
            basis[pl.ds(pl.multiple_of(first * rank, rows), rows), :],
            scaled_t[...],
            expert[...],
            acc,
        )

    def from_z(s):
        z_copy[s].wait_recv()
        x_copy[s] = send(piece(column[s], y), piece(column[s], y), x_peer, xs, s)
        to_y(s - 1, column[s])
        to_c(4 * s, column[s], y)

    def from_x(s):
        x_copy[s].wait_recv()
        to_y(nz + s - 2, across[s])
        to_c(4 * s + 1, across[s], y)

    for s in order[:-1]:
        from_z(s)
    x_copy[0].wait_recv()
    c_copy[1] = send(whole(across[0]), whole(across[0]), c_peer, cs, 1)
    for s in order[-1:]:
        from_z(s)
    c_copy[0].wait_recv()
    c_copy[1].wait_recv()
    quad(0)
    for s in order:
        from_x(s)
    for s in order:
        y_copy[s - 1].wait_recv()
        to_c(4 * s + 2, column[s], 1 - y)
    for s in order:
        y_copy[nz + s - 2].wait_recv()
        to_c(4 * s + 3, across[s], 1 - y)
    for s in order:
        for i in range(4):
            c_copy[4 * s + i].wait_recv()
        quad(s)
    write_out(acc, out_ref, rank)
    for copy in started:
        copy.wait_send()


def local_kernel(
    counts_ref, cot, hidden, gates, ids, out_basis, basis, out_ref, scaled_t, expert, acc
):
    rank = out_basis.shape[0]
    experts = out_ref.shape[1]
    scaled_t[...], expert[...] = route_columns(
        cot[...], out_basis[...], gates[...], ids[...], counts_ref[0]
    )

    @pl.loop(0, experts // 4)
    def _(j):
        group_sums(
            4 * j,
            hidden[...],
            basis[pl.ds(pl.multiple_of(4 * j * rank, 4 * rank), 4 * rank), :],
            scaled_t[...],
            expert[...],
            acc,
        )

    write_out(acc, out_ref, rank)


def on_device(cotangent, hidden, gates, expert_ids, counts, proj_out, proj_in):
    tokens, top = expert_ids.shape
    routes = tokens * top
    model = cotangent.shape[1]
    rank = proj_out.shape[0]
    width = hidden.shape[2]
    experts = lax.axis_size("expert")
    dp = lax.axis_size("dp")
    bf16 = jnp.bfloat16
    if dp > 1:
        proj_out = lax.all_gather(proj_out, "dp", axis=1, tiled=True)
        proj_in = lax.all_gather(proj_in, "dp", axis=2, tiled=True)
    hidden = hidden.reshape(routes, width)
    gates, expert_ids = gates.T, expert_ids.T
    out_shape = jax.ShapeDtypeStruct((1, experts, rank * rank), bf16)
    tail = [
        pltpu.VMEM((rank, routes), bf16),
        pltpu.VMEM((routes, 2 * rank), jnp.float32),
        pltpu.VMEM((experts * rank, 2 * rank), jnp.float32),
    ]
    cost = pl.CostEstimate(
        flops=2 * routes * experts * rank * (width + rank),
        bytes_accessed=2 * (tokens * model + routes * width + experts * rank * width),
        transcendentals=0,
    )
    smem = pl.BlockSpec(memory_space=pltpu.SMEM)
    vmem = pl.BlockSpec(memory_space=pltpu.VMEM)
    anywhere = pl.BlockSpec(memory_space=pl.ANY)
    if experts != 16 or dp > 1 or lax.axis_size("groups") != 2:
        basis = lax.all_gather(proj_in.reshape(rank, width), "expert", axis=0, tiled=True)
        return pl.pallas_call(
            local_kernel,
            out_shape=out_shape,
            in_specs=[smem] + [vmem] * 6,
            out_specs=vmem,
            scratch_shapes=tail,
            cost_estimate=cost,
            compiler_params=pltpu.CompilerParams(vmem_limit_bytes=48 << 20),
        )(counts, cotangent, hidden, gates, expert_ids, proj_out, basis)
    parts = (experts // 4, 2, 2)
    dma = pltpu.SemaphoreType.DMA
    nz = parts[0]
    return pl.pallas_call(
        functools.partial(ring_kernel, parts),
        out_shape=out_shape,
        in_specs=[anywhere] * 7,
        out_specs=vmem,
        scratch_shapes=[
            pltpu.SMEM((1,), jnp.int32),
            pltpu.VMEM((tokens, model), bf16),
            pltpu.VMEM((routes, width), bf16),
            pltpu.VMEM((top, tokens), bf16),
            pltpu.VMEM((top, tokens), jnp.int32),
            pltpu.VMEM((rank, model), bf16),
            pltpu.VMEM((experts * rank, width), bf16),
        ]
        + tail
        + [
            dma((7,)),
            dma((nz - 1,)),
            dma((nz - 1,)),
            dma((nz,)),
            dma((nz,)),
            dma((2 * nz - 2,)),
            dma((2 * nz - 2,)),
            dma((4 * nz,)),
            dma((4 * nz,)),
        ],
        cost_estimate=cost,
        compiler_params=pltpu.CompilerParams(
            collective_id=0, has_side_effects=True, vmem_limit_bytes=63 << 20
        ),
    )(counts, cotangent, hidden, gates, expert_ids, proj_out, proj_in.reshape(rank, width))


def solution(mesh):
    rows = ("groups", "expert", "dp")
    placed = (
        P(rows, None),
        P(rows, None, None),
        P(rows, None),
        P(rows, None),
        P(rows),
        P(None, "dp"),
        P("expert", None, "dp"),
    )
    return jax.shard_map(
        on_device,
        mesh=mesh,
        in_specs=placed,
        out_specs=P(rows, None, None),
        check_vma=False,
    )
```

```python
import functools

import jax
import jax.numpy as jnp
from jax import lax
from jax.experimental import pallas as pl
from jax.experimental.pallas import tpu as pltpu
from jax.sharding import PartitionSpec as P

ACROSS = (((1,), (1,)), ((), ()))


def route_columns(cot, basis_out, gates, ids, used):
    top, tokens = gates.shape
    routes = tokens * top
    rank = basis_out.shape[0]
    projected = lax.dot_general(cot, basis_out, ACROSS, preferred_element_type=jnp.float32)
    spread = (
        lax.broadcasted_iota(jnp.int32, (routes, tokens), 0) // top
        == lax.broadcasted_iota(jnp.int32, (routes, tokens), 1)
    ).astype(jnp.bfloat16)
    own = lax.broadcasted_iota(jnp.int32, (routes, top), 0) % top == lax.broadcasted_iota(
        jnp.int32, (routes, top), 1
    )

    def column(values):
        wide = lax.dot_general(spread, values, ACROSS, preferred_element_type=jnp.float32)
        return jnp.sum(jnp.where(own, wide, 0.0), axis=1, keepdims=True)

    gate = column(gates)
    expert = column(ids.astype(jnp.float32).astype(jnp.bfloat16))
    live = lax.broadcasted_iota(jnp.int32, (routes, 1), 0) // top < used
    weight = jnp.where(live, gate, 0.0)
    rows = jnp.broadcast_to(projected[:, None, :], (tokens, top, rank)).reshape(routes, rank)
    scaled = weight * rows
    return scaled.T.astype(jnp.bfloat16), jnp.broadcast_to(expert, (routes, 2 * rank))


def group_sums(first, hidden, basis, scaled_t, expert, acc_ref):
    rank = scaled_t.shape[0]
    routes = hidden.shape[0]
    pair = 2 * rank
    reduced = lax.dot_general(hidden, basis, ACROSS, preferred_element_type=jnp.float32)
    lane = lax.broadcasted_iota(jnp.int32, (routes, pair), 1)
    left = lax.broadcasted_iota(jnp.int32, (rank, pair), 1) < rank
    kept = []
    for p in range(basis.shape[0] // pair):
        names = (first + 2 * p + lane // rank).astype(jnp.float32)
        kept.append(jnp.where(expert == names, reduced[:, p * pair : (p + 1) * pair], 0.0))
    kept = jnp.concatenate(kept, axis=1).astype(jnp.bfloat16)
    sums = jnp.dot(scaled_t, kept, preferred_element_type=jnp.float32)
    for p in range(basis.shape[0] // pair):
        part = sums[:, p * pair : (p + 1) * pair]
        turned = pltpu.roll(part, rank, 1)
        at = pl.multiple_of((first + 2 * p) * rank, pair)
        acc_ref[pl.ds(at, rank), :] = jnp.where(left, part, turned)
        acc_ref[pl.ds(at + rank, rank), :] = jnp.where(left, turned, part)


def write_out(acc_ref, out_ref, rank):
    experts = out_ref.shape[1]
    left = lax.broadcasted_iota(jnp.int32, (experts, 2 * rank), 1) < rank
    for c in range(rank // 2):
        even = acc_ref[pl.ds(2 * c, experts, stride=rank), :]
        odd = acc_ref[pl.ds(2 * c + 1, experts, stride=rank), :]
        out_ref[0, :, pl.ds(c * 2 * rank, 2 * rank)] = jnp.where(left, even, odd).astype(out_ref.dtype)


def ring_kernel(
    parts,
    counts_ref, cot_ref, hidden_ref, gates_ref, ids_ref, out_basis_ref, in_basis_ref,
    out_ref,
    counts, cot, hidden, gates, ids, out_basis, basis, scaled_t, expert, acc,
    load_sem, z_send, z_recv, x_send, x_recv, y_send, y_recv, c_send, c_recv,
):
    nz, nx, nc = parts
    rank, width = in_basis_ref.shape
    half = rank // 2
    me = lax.axis_index("expert")
    y = lax.axis_index("groups")
    z, x, c = me // (nx * nc), (me // nc) % nx, me % nc

    def place(pz, px, pc):
        return (pz * nx + px) * nc + pc

    def whole(e):
        return basis.at[pl.ds(pl.multiple_of(e * rank, rank), rank), :]

    def piece(e, h):
        return basis.at[pl.ds(pl.multiple_of(e * rank + h * half, half), half), :]

    loads = [
        pltpu.make_async_copy(src, dst, load_sem.at[i])
        for i, (src, dst) in enumerate(
            [
                (in_basis_ref, whole(me)),
                (cot_ref, cot),
                (out_basis_ref, out_basis),
                (gates_ref, gates),
                (ids_ref, ids),
                (counts_ref, counts),
                (hidden_ref, hidden),
            ]
        )
    ]
    for load in loads:
        load.start()

    x_peer = {"expert": place(z, 1 - x, c)}
    c_peer = {"expert": place(z, x, 1 - c)}
    y_peer = {"groups": 1 - y}
    d_peer = {"groups": 1 - y, "expert": place(z, 1 - x, c)}
    along = [z, z + 1 - 2 * (z % 2), (z + 2) % nz, nz - 1 - z]
    z_peer = {s: {"expert": place(along[s], x, c)} for s in range(1, nz)}
    peers = list(z_peer.values()) + [x_peer, y_peer, c_peer, d_peer]
    barrier = pltpu.get_barrier_semaphore()
    for peer in peers:
        pl.semaphore_signal(barrier, inc=1, device_id=peer, device_id_type=pl.DeviceIdType.MESH)
    pl.semaphore_wait(barrier, len(peers))

    started = []

    def send(source, target, peer, sems, i):
        copy = pltpu.make_async_remote_copy(
            src_ref=source,
            dst_ref=target,
            send_sem=sems[0].at[i],
            recv_sem=sems[1].at[i],
            device_id=peer,
            device_id_type=pl.DeviceIdType.MESH,
        )
        copy.start()
        started.append(copy)
        return copy

    zs, xs, ys, cs = (z_send, z_recv), (x_send, x_recv), (y_send, y_recv), (c_send, c_recv)
    column = [place(along[s], x, c) for s in range(nz)]
    across = [place(along[s], 1 - x, c) for s in range(nz)]
    order, diagonal = [1, 2, 3], []
    z_copy, x_copy, y_copy, c_copy = {}, {}, {}, {}

    def to_y(i, e, peer):
        y_copy[i] = send(piece(e, y), piece(e, y), peer, ys, i)

    def to_c(i, e, h):
        c_copy[i] = send(piece(e, h), piece(e, h), c_peer, cs, i)

    mine = in_basis_ref.at[pl.ds(pl.multiple_of(y * half, half), half), :]
    for s in order:
        z_copy[s] = send(mine, piece(me, y), z_peer[s], zs, s - 1)
    x_copy[0] = send(in_basis_ref, whole(me), x_peer, xs, 0)
    c_copy[0] = send(in_basis_ref, whole(me), c_peer, cs, 0)

    for load in loads[1:6]:
        load.wait()
    scaled_t[...], expert[...] = route_columns(
        cot[...], out_basis[...], gates[...], ids[...], counts[0]
    )
    loads[6].wait()
    loads[0].wait()

    def quad(s):
        first = along[s] * (nx * nc)
        rows = nx * nc * rank
        group_sums(
            first,
            hidden[...],
            basis[pl.ds(pl.multiple_of(first * rank, rows), rows), :],
            scaled_t[...],
            expert[...],
            acc,
        )

    def from_z(s):
        z_copy[s].wait_recv()
        x_copy[s] = send(piece(column[s], y), piece(column[s], y), x_peer, xs, s)
        to_y(s - 1, column[s], y_peer)
        if s in diagonal:
            to_y(nz + s - 2, column[s], d_peer)
        to_c(4 * s, column[s], y)

    def from_x(s):
        x_copy[s].wait_recv()
        if s not in diagonal:
            to_y(nz + s - 2, across[s], y_peer)
        to_c(4 * s + 1, across[s], y)

    def from_y(s):
        y_copy[s - 1].wait_recv()
        to_c(4 * s + 2, column[s], 1 - y)

    def from_far(s):
        y_copy[nz + s - 2].wait_recv()
        to_c(4 * s + 3, across[s], 1 - y)

    def finish(s):
        for i in range(4):
            c_copy[4 * s + i].wait_recv()
        quad(s)

    for s in order[:-1]:
        from_z(s)
    x_copy[0].wait_recv()
    c_copy[1] = send(whole(across[0]), whole(across[0]), c_peer, cs, 1)
    from_z(order[-1])
    c_copy[0].wait_recv()
    c_copy[1].wait_recv()
    quad(0)
    for s in order:
        from_x(s)
        from_y(s)
    for s in order[:-1]:
        from_far(s)
    finish(order[0])
    from_far(order[-1])
    for s in order[1:]:
        finish(s)
    write_out(acc, out_ref, rank)
    for copy in started:
        copy.wait_send()


def local_kernel(
    counts_ref, cot, hidden, gates, ids, out_basis, basis, out_ref, scaled_t, expert, acc
):
    rank = out_basis.shape[0]
    experts = out_ref.shape[1]
    scaled_t[...], expert[...] = route_columns(
        cot[...], out_basis[...], gates[...], ids[...], counts_ref[0]
    )

    @pl.loop(0, experts // 4)
    def _(j):
        group_sums(
            4 * j,
            hidden[...],
            basis[pl.ds(pl.multiple_of(4 * j * rank, 4 * rank), 4 * rank), :],
            scaled_t[...],
            expert[...],
            acc,
        )

    write_out(acc, out_ref, rank)


def on_device(cotangent, hidden, gates, expert_ids, counts, proj_out, proj_in):
    tokens, top = expert_ids.shape
    routes = tokens * top
    model = cotangent.shape[1]
    rank = proj_out.shape[0]
    width = hidden.shape[2]
    experts = lax.axis_size("expert")
    dp = lax.axis_size("dp")
    bf16 = jnp.bfloat16
    if dp > 1:
        proj_out = lax.all_gather(proj_out, "dp", axis=1, tiled=True)
        proj_in = lax.all_gather(proj_in, "dp", axis=2, tiled=True)
    hidden = hidden.reshape(routes, width)
    gates, expert_ids = gates.T, expert_ids.T
    out_shape = pltpu.VMEM((1, experts, rank * rank), bf16)
    tail = [
        pltpu.VMEM((rank, routes), bf16),
        pltpu.VMEM((routes, 2 * rank), jnp.float32),
        pltpu.VMEM((experts * rank, 2 * rank), jnp.float32),
    ]
    cost = pl.CostEstimate(
        flops=2 * routes * experts * rank * (width + rank),
        bytes_accessed=2 * (tokens * model + routes * width + experts * rank * width),
        transcendentals=0,
    )
    smem = pl.BlockSpec(memory_space=pltpu.SMEM)
    vmem = pl.BlockSpec(memory_space=pltpu.VMEM)
    anywhere = pl.BlockSpec(memory_space=pl.ANY)
    if experts != 16 or dp > 1 or lax.axis_size("groups") != 2:
        basis = lax.all_gather(proj_in.reshape(rank, width), "expert", axis=0, tiled=True)
        return pl.pallas_call(
            local_kernel,
            out_shape=out_shape,
            in_specs=[smem] + [vmem] * 6,
            out_specs=vmem,
            scratch_shapes=tail,
            cost_estimate=cost,
            compiler_params=pltpu.CompilerParams(vmem_limit_bytes=48 << 20),
        )(counts, cotangent, hidden, gates, expert_ids, proj_out, basis)
    parts = (experts // 4, 2, 2)
    dma = pltpu.SemaphoreType.DMA
    nz = parts[0]
    return pl.pallas_call(
        functools.partial(ring_kernel, parts),
        out_shape=out_shape,
        in_specs=[anywhere] * 7,
        out_specs=vmem,
        scratch_shapes=[
            pltpu.SMEM((1,), jnp.int32),
            pltpu.VMEM((tokens, model), bf16),
            pltpu.VMEM((routes, width), bf16),
            pltpu.VMEM((top, tokens), bf16),
            pltpu.VMEM((top, tokens), jnp.int32),
            pltpu.VMEM((rank, model), bf16),
            pltpu.VMEM((experts * rank, width), bf16),
        ]
        + tail
        + [
            dma((7,)),
            dma((nz - 1,)),
            dma((nz - 1,)),
            dma((nz,)),
            dma((nz,)),
            dma((2 * nz - 2,)),
            dma((2 * nz - 2,)),
            dma((4 * nz,)),
            dma((4 * nz,)),
        ],
        cost_estimate=cost,
        compiler_params=pltpu.CompilerParams(
            collective_id=0, has_side_effects=True, vmem_limit_bytes=63 << 20
        ),
    )(counts, cotangent, hidden, gates, expert_ids, proj_out, proj_in.reshape(rank, width))


def solution(mesh):
    rows = ("groups", "expert", "dp")
    placed = (
        P(rows, None),
        P(rows, None, None),
        P(rows, None),
        P(rows, None),
        P(rows),
        P(None, "dp"),
        P("expert", None, "dp"),
    )
    return jax.shard_map(
        on_device,
        mesh=mesh,
        in_specs=placed,
        out_specs=P(rows, None, None),
        check_vma=False,
    )
```

```python
import functools

import jax
import jax.numpy as jnp
from jax import lax
from jax.experimental import pallas as pl
from jax.experimental.pallas import tpu as pltpu
from jax.sharding import PartitionSpec as P

ACROSS = (((1,), (1,)), ((), ()))


def route_columns(cot, basis_out, gates, ids, used):
    top, tokens = gates.shape
    routes = tokens * top
    rank = basis_out.shape[0]
    projected = lax.dot_general(cot, basis_out, ACROSS, preferred_element_type=jnp.float32)
    spread = (
        lax.broadcasted_iota(jnp.int32, (routes, tokens), 0) // top
        == lax.broadcasted_iota(jnp.int32, (routes, tokens), 1)
    ).astype(jnp.bfloat16)
    own = lax.broadcasted_iota(jnp.int32, (routes, top), 0) % top == lax.broadcasted_iota(
        jnp.int32, (routes, top), 1
    )

    def column(values):
        wide = lax.dot_general(spread, values, ACROSS, preferred_element_type=jnp.float32)
        return jnp.sum(jnp.where(own, wide, 0.0), axis=1, keepdims=True)

    gate = column(gates)
    expert = column(ids.astype(jnp.float32).astype(jnp.bfloat16))
    live = lax.broadcasted_iota(jnp.int32, (routes, 1), 0) // top < used
    weight = jnp.where(live, gate, 0.0)
    rows = jnp.broadcast_to(projected[:, None, :], (tokens, top, rank)).reshape(routes, rank)
    scaled = weight * rows
    return scaled.T.astype(jnp.bfloat16), jnp.broadcast_to(expert, (routes, 2 * rank))


def group_sums(first, hidden, basis, scaled_t, expert, acc_ref):
    rank = scaled_t.shape[0]
    routes = hidden.shape[0]
    pair = 2 * rank
    reduced = lax.dot_general(hidden, basis, ACROSS, preferred_element_type=jnp.float32)
    lane = lax.broadcasted_iota(jnp.int32, (routes, pair), 1)
    left = lax.broadcasted_iota(jnp.int32, (rank, pair), 1) < rank
    kept = []
    for p in range(basis.shape[0] // pair):
        names = (first + 2 * p + lane // rank).astype(jnp.float32)
        kept.append(jnp.where(expert == names, reduced[:, p * pair : (p + 1) * pair], 0.0))
    kept = jnp.concatenate(kept, axis=1).astype(jnp.bfloat16)
    sums = jnp.dot(scaled_t, kept, preferred_element_type=jnp.float32)
    for p in range(basis.shape[0] // pair):
        part = sums[:, p * pair : (p + 1) * pair]
        turned = pltpu.roll(part, rank, 1)
        at = pl.multiple_of((first + 2 * p) * rank, pair)
        acc_ref[pl.ds(at, rank), :] = jnp.where(left, part, turned)
        acc_ref[pl.ds(at + rank, rank), :] = jnp.where(left, turned, part)


def write_out(acc_ref, out_ref, rank):
    experts = out_ref.shape[1]
    left = lax.broadcasted_iota(jnp.int32, (experts, 2 * rank), 1) < rank
    for c in range(rank // 2):
        even = acc_ref[pl.ds(2 * c, experts, stride=rank), :]
        odd = acc_ref[pl.ds(2 * c + 1, experts, stride=rank), :]
        out_ref[0, :, pl.ds(c * 2 * rank, 2 * rank)] = jnp.where(left, even, odd).astype(out_ref.dtype)


def ring_kernel(
    parts,
    counts_ref, cot_ref, hidden_ref, gates_ref, ids_ref, out_basis_ref, in_basis_ref,
    out_ref,
    counts, cot, hidden, gates, ids, out_basis, basis, scaled_t, expert, acc,
    load_sem, z_send, z_recv, x_send, x_recv, y_send, y_recv, c_send, c_recv,
):
    nz, nx, nc = parts
    rank, width = in_basis_ref.shape
    half = rank // 2
    me = lax.axis_index("expert")
    y = lax.axis_index("groups")
    z, x, c = me // (nx * nc), (me // nc) % nx, me % nc

    def place(pz, px, pc):
        return (pz * nx + px) * nc + pc

    def whole(e):
        return basis.at[pl.ds(pl.multiple_of(e * rank, rank), rank), :]

    def piece(e, h):
        return basis.at[pl.ds(pl.multiple_of(e * rank + h * half, half), half), :]

    loads = [
        pltpu.make_async_copy(src, dst, load_sem.at[i])
        for i, (src, dst) in enumerate(
            [
                (in_basis_ref, whole(me)),
                (cot_ref, cot),
                (out_basis_ref, out_basis),
                (gates_ref, gates),
                (ids_ref, ids),
                (counts_ref, counts),
                (hidden_ref, hidden),
            ]
        )
    ]
    for load in loads:
        load.start()

    x_peer = {"expert": place(z, 1 - x, c)}
    c_peer = {"expert": place(z, x, 1 - c)}
    y_peer = {"groups": 1 - y}
    d_peer = {"groups": 1 - y, "expert": place(z, 1 - x, c)}
    along = [z, z + 1 - 2 * (z % 2), (z + 2) % nz, nz - 1 - z]
    z_peer = {s: {"expert": place(along[s], x, c)} for s in range(1, nz)}
    peers = list(z_peer.values()) + [x_peer, y_peer, c_peer, d_peer]
    barrier = pltpu.get_barrier_semaphore()
    for peer in peers:
        pl.semaphore_signal(barrier, inc=1, device_id=peer, device_id_type=pl.DeviceIdType.MESH)
    pl.semaphore_wait(barrier, len(peers))

    started = []

    def send(source, target, peer, sems, i):
        copy = pltpu.make_async_remote_copy(
            src_ref=source,
            dst_ref=target,
            send_sem=sems[0].at[i],
            recv_sem=sems[1].at[i],
            device_id=peer,
            device_id_type=pl.DeviceIdType.MESH,
        )
        copy.start()
        started.append(copy)
        return copy

    zs, xs, ys, cs = (z_send, z_recv), (x_send, x_recv), (y_send, y_recv), (c_send, c_recv)
    column = [place(along[s], x, c) for s in range(nz)]
    across = [place(along[s], 1 - x, c) for s in range(nz)]
    order, diagonal = [1, 2, 3], []
    z_copy, x_copy, y_copy, c_copy = {}, {}, {}, {}

    def to_y(i, e, peer):
        y_copy[i] = send(piece(e, y), piece(e, y), peer, ys, i)

    def to_c(i, e, h):
        c_copy[i] = send(piece(e, h), piece(e, h), c_peer, cs, i)

    mine = in_basis_ref.at[pl.ds(pl.multiple_of(y * half, half), half), :]
    for s in order:
        z_copy[s] = send(mine, piece(me, y), z_peer[s], zs, s - 1)
    x_copy[0] = send(in_basis_ref, whole(me), x_peer, xs, 0)
    c_copy[0] = send(in_basis_ref, whole(me), c_peer, cs, 0)

    for load in loads[1:6]:
        load.wait()
    scaled_t[...], expert[...] = route_columns(
        cot[...], out_basis[...], gates[...], ids[...], counts[0]
    )
    loads[6].wait()
    loads[0].wait()

    def quad(s):
        first = along[s] * (nx * nc)
        rows = nx * nc * rank
        group_sums(
            first,
            hidden[...],
            basis[pl.ds(pl.multiple_of(first * rank, rows), rows), :],
            scaled_t[...],
            expert[...],
            acc,
        )

    def from_z(s):
        z_copy[s].wait_recv()
        x_copy[s] = send(piece(column[s], y), piece(column[s], y), x_peer, xs, s)
        to_y(s - 1, column[s], y_peer)
        if s in diagonal:
            to_y(nz + s - 2, column[s], d_peer)
        to_c(4 * s, column[s], y)

    def from_x(s):
        x_copy[s].wait_recv()
        if s not in diagonal:
            to_y(nz + s - 2, across[s], y_peer)
        to_c(4 * s + 1, across[s], y)

    def from_y(s):
        y_copy[s - 1].wait_recv()
        to_c(4 * s + 2, column[s], 1 - y)

    def from_far(s):
        y_copy[nz + s - 2].wait_recv()
        to_c(4 * s + 3, across[s], 1 - y)

    def finish(s):
        for i in range(4):
            c_copy[4 * s + i].wait_recv()
        quad(s)

    for s in order[:-1]:
        from_z(s)
    x_copy[0].wait_recv()
    c_copy[1] = send(whole(across[0]), whole(across[0]), c_peer, cs, 1)
    from_z(order[-1])
    c_copy[0].wait_recv()
    c_copy[1].wait_recv()
    for s in order:
        from_x(s)
        from_y(s)
        if s == order[0]:
            quad(0)
    for s in order[:-1]:
        from_far(s)
    finish(order[0])
    from_far(order[-1])
    for s in order[1:]:
        finish(s)
    write_out(acc, out_ref, rank)
    for copy in started:
        copy.wait_send()


def local_kernel(
    counts_ref, cot, hidden, gates, ids, out_basis, basis, out_ref, scaled_t, expert, acc
):
    rank = out_basis.shape[0]
    experts = out_ref.shape[1]
    scaled_t[...], expert[...] = route_columns(
        cot[...], out_basis[...], gates[...], ids[...], counts_ref[0]
    )

    @pl.loop(0, experts // 4)
    def _(j):
        group_sums(
            4 * j,
            hidden[...],
            basis[pl.ds(pl.multiple_of(4 * j * rank, 4 * rank), 4 * rank), :],
            scaled_t[...],
            expert[...],
            acc,
        )

    write_out(acc, out_ref, rank)


def on_device(cotangent, hidden, gates, expert_ids, counts, proj_out, proj_in):
    tokens, top = expert_ids.shape
    routes = tokens * top
    model = cotangent.shape[1]
    rank = proj_out.shape[0]
    width = hidden.shape[2]
    experts = lax.axis_size("expert")
    dp = lax.axis_size("dp")
    bf16 = jnp.bfloat16
    if dp > 1:
        proj_out = lax.all_gather(proj_out, "dp", axis=1, tiled=True)
        proj_in = lax.all_gather(proj_in, "dp", axis=2, tiled=True)
    hidden = hidden.reshape(routes, width)
    gates, expert_ids = gates.T, expert_ids.T
    out_shape = pltpu.VMEM((1, experts, rank * rank), bf16)
    tail = [
        pltpu.VMEM((rank, routes), bf16),
        pltpu.VMEM((routes, 2 * rank), jnp.float32),
        pltpu.VMEM((experts * rank, 2 * rank), jnp.float32),
    ]
    cost = pl.CostEstimate(
        flops=2 * routes * experts * rank * (width + rank),
        bytes_accessed=2 * (tokens * model + routes * width + experts * rank * width),
        transcendentals=0,
    )
    smem = pl.BlockSpec(memory_space=pltpu.SMEM)
    vmem = pl.BlockSpec(memory_space=pltpu.VMEM)
    anywhere = pl.BlockSpec(memory_space=pl.ANY)
    if experts != 16 or dp > 1 or lax.axis_size("groups") != 2:
        basis = lax.all_gather(proj_in.reshape(rank, width), "expert", axis=0, tiled=True)
        return pl.pallas_call(
            local_kernel,
            out_shape=out_shape,
            in_specs=[smem] + [vmem] * 6,
            out_specs=vmem,
            scratch_shapes=tail,
            cost_estimate=cost,
            compiler_params=pltpu.CompilerParams(vmem_limit_bytes=48 << 20),
        )(counts, cotangent, hidden, gates, expert_ids, proj_out, basis)
    parts = (experts // 4, 2, 2)
    dma = pltpu.SemaphoreType.DMA
    nz = parts[0]
    return pl.pallas_call(
        functools.partial(ring_kernel, parts),
        out_shape=out_shape,
        in_specs=[anywhere] * 7,
        out_specs=vmem,
        scratch_shapes=[
            pltpu.SMEM((1,), jnp.int32),
            pltpu.VMEM((tokens, model), bf16),
            pltpu.VMEM((routes, width), bf16),
            pltpu.VMEM((top, tokens), bf16),
            pltpu.VMEM((top, tokens), jnp.int32),
            pltpu.VMEM((rank, model), bf16),
            pltpu.VMEM((experts * rank, width), bf16),
        ]
        + tail
        + [
            dma((7,)),
            dma((nz - 1,)),
            dma((nz - 1,)),
            dma((nz,)),
            dma((nz,)),
            dma((2 * nz - 2,)),
            dma((2 * nz - 2,)),
            dma((4 * nz,)),
            dma((4 * nz,)),
        ],
        cost_estimate=cost,
        compiler_params=pltpu.CompilerParams(
            collective_id=0, has_side_effects=True, vmem_limit_bytes=63 << 20
        ),
    )(counts, cotangent, hidden, gates, expert_ids, proj_out, proj_in.reshape(rank, width))


def solution(mesh):
    rows = ("groups", "expert", "dp")
    placed = (
        P(rows, None),
        P(rows, None, None),
        P(rows, None),
        P(rows, None),
        P(rows),
        P(None, "dp"),
        P("expert", None, "dp"),
    )
    return jax.shard_map(
        on_device,
        mesh=mesh,
        in_specs=placed,
        out_specs=P(rows, None, None),
        check_vma=False,
    )
```
